32 devices in a mesh: dp: 4 (over x, core), ctx: 4 (over z), tensor: 2 (over y).
Axes of the slice: x: 2, y: 2, z: 4, core: 2. Of those that a mesh axis runs over, the one named last changes fastest.
Arguments:
- hidden_in: float32 [8, 2048, 1024], P('dp', 'ctx', 'tensor'), may hold values from -6 to 6
- cotangent: float32 [8, 2048, 1024], P('dp', 'ctx', 'tensor'), may hold values from -6 to 6
- lengths: int32 [8, 8], P('dp'), may hold values from 1 to 128, 768 in all within a row
- w_query: bfloat16 [2, 1024, 1024], P(None, 'dp', 'tensor'), may hold values from -0.1875 to 0.1875
- w_key: bfloat16 [2, 1024, 1024], P(None, 'dp', 'tensor'), may hold values from -0.1875 to 0.1875
- w_value: bfloat16 [2, 1024, 1024], P(None, 'dp', 'tensor'), may hold values from -0.1875 to 0.1875
- w_output: bfloat16 [2, 1024, 1024], P(None, 'dp', 'tensor'), may hold values from -1 to 1
- w_up: bfloat16 [2, 1024, 8192], P(None, 'dp', 'tensor'), may hold values from -0.1875 to 0.1875
- w_down: bfloat16 [2, 1024, 8192], P(None, 'dp', 'tensor'), may hold values from -0.0625 to 0.0625
- norm_params: bfloat16 [2, 4, 1024], P(None, 'dp', 'tensor'), may hold values from 0.5 to 1.5
Outputs:
- output: float32 [8, 2048, 1024], P('dp', 'ctx', 'tensor')
- grad_input: float32 [8, 2048, 1024], P('dp', 'ctx', 'tensor')
- grad_query: float32 [2, 1024, 1024], P(None, 'dp', 'tensor')
- grad_key: float32 [2, 1024, 1024], P(None, 'dp', 'tensor')
- grad_value: float32 [2, 1024, 1024], P(None, 'dp', 'tensor')
- grad_output: float32 [2, 1024, 1024], P(None, 'dp', 'tensor')
- grad_up: float32 [2, 1024, 8192], P(None, 'dp', 'tensor')
- grad_down: float32 [2, 1024, 8192], P(None, 'dp', 'tensor')
- grad_norms: float32 [2, 4, 1024], P(None, 'dp', 'tensor')
The draws below stay inside these ranges and needn't reach their ends.
Inputs may be any that keep to these rules, and one draw needn't show every extreme that they name: `lengths`: A group's entries sum to 768, and one of them equals 128.
All inputs are finite; a program needn't handle non-finite values.
Results may differ from the reference program's by a relative error of at most 0.023.
Values may be sent and summed in bfloat16 or wider, within the bound.
No kernel may reach another device: no remote copies, remote signals or barrier semaphores. Data moves between devices by JAX's collectives and lax.ppermute only.
A program may use at most 448 MiB of HBM per device.

```python
import math
import jax
import jax.numpy as jnp
import numpy as np
from jax import lax

D = 1024
HEADS = 16
HEAD_DIM = 64
FF = 8192
LAYERS = 2
PROMPT = 1024
CONTS = 8
CONT = 128
GROUP = 2048
GROUPS = 8


def level_of(key, shape, split, smallest, high):
    def one(axis_at, blocks):
        steps = jax.random.uniform(jax.random.fold_in(jax.random.fold_in(key, 6), axis_at), (blocks,), jnp.float32, smallest / len(split), high / len(split))
        return jnp.repeat(jnp.exp(steps), shape[axis_at] // blocks).reshape((-1,) + (1,) * (len(shape) - axis_at - 1))

    gain = one(*split[0])
    for cut in split[1:]:
        gain = gain * one(*cut)
    return gain


def profile(number_of, total, limit, lean):
    portions = [(1 << 20) // math.isqrt(standing ** lean) + 1 for standing in range(2, number_of + 1)]
    spare, holding = total - limit - (number_of - 1), [1] * (number_of - 1)
    while spare > 0:
        movable = [i for i in range(number_of - 1) if holding[i] < limit]
        pool, left = sum([portions[i] for i in movable]), spare
        for i in movable:
            addition = min(limit - holding[i], max(1, left * portions[i] // pool), spare)
            holding[i] = holding[i] + addition
            spare = spare - addition
    return np.array([limit] + holding)


def uneven(stream_key, amount, total, limit, lean):
    if amount == 2:
        one = jax.random.randint(stream_key, (), max(1, total - limit), min(limit, total - 1) + 1)
        return jnp.stack([one, total - one])
    sizes = jnp.asarray(profile(amount, total, limit, lean), jnp.int32)
    twos = (amount - 1) // 2
    donor, sink = sizes[1:1 + 2 * twos:2], sizes[2:2 + 2 * twos:2]
    slack = jnp.minimum(donor - 1, limit - sink)
    passed = jax.random.randint(jax.random.fold_in(stream_key, 1), (twos,), 0, 1 << 20) % (slack + 1)
    sizes = sizes.at[1:1 + 2 * twos:2].set(donor - passed).at[2:2 + 2 * twos:2].set(sink + passed)
    return sizes[jax.random.permutation(jax.random.fold_in(stream_key, 2), amount)]


def noise(stream_key, shape, width, reach, cuts=(), kind=jnp.bfloat16):
    entries = width * jax.random.normal(stream_key, shape, jnp.float32)
    if cuts:
        entries = entries * level_of(stream_key, shape, cuts, -0.22, 0.18)
    return jnp.clip(entries, -reach, reach).astype(kind)


def setup_inputs(seed: int = 0) -> dict:
    key_list = jax.random.split(jax.random.key(seed), 11)
    return {
        "hidden_in": noise(key_list[0], (GROUPS, GROUP, D), 1.0, 6.0, ((0, 4), (1, 4), (2, 2)), jnp.float32),
        "cotangent": noise(key_list[1], (GROUPS, GROUP, D), 1.0, 6.0, ((0, 4), (1, 4), (2, 2)), jnp.float32),
        "lengths": jax.vmap(lambda own: uneven(own, CONTS, 6 * CONT, CONT, 2))(jax.random.split(key_list[2], GROUPS)).reshape((GROUPS, CONTS)).astype(jnp.int32),
        "w_query": noise(key_list[3], (LAYERS, D, D), D ** -0.5, 0.1875, ((1, 4), (2, 2))),
        "w_key": noise(key_list[4], (LAYERS, D, D), D ** -0.5, 0.1875, ((1, 4), (2, 2))),
        "w_value": noise(key_list[5], (LAYERS, D, D), D ** -0.5, 0.1875, ((1, 4), (2, 2))),
        "w_output": noise(key_list[6], (LAYERS, D, D), (D * 64 // GROUP) ** -0.5, 1.0, ((1, 4), (2, 2))),
        "w_up": noise(key_list[7], (LAYERS, D, FF), D ** -0.5, 0.1875, ((1, 4), (2, 2))),
        "w_down": noise(key_list[8], (LAYERS, D, FF), FF ** -0.5, 0.0625, ((1, 4), (2, 2))),
        "norm_params": jnp.clip(0.5 + 1.0 * jax.random.uniform(key_list[9], (LAYERS, 4, D), jnp.float32) ** level_of(key_list[9], (LAYERS, 4, D), ((1, 4), (2, 2)), -0.2, 0.2), 0.5, 1.5).astype(jnp.bfloat16),
    }


@jax.custom_vjp
def low(v):
    return lax.optimization_barrier(v.astype(jnp.bfloat16)).astype(jnp.float32)

@jax.custom_vjp
def low_back(v):
    return v

def low_keep(v):
    return (low(v), None)

def low_pass(kept, grad):
    return (grad,)

def back_keep(v):
    return (v, None)

def back_low(kept, grad):
    return (low(grad),)
low.defvjp(low_keep, low_pass)
low_back.defvjp(back_keep, back_low)
highest = lax.Precision.HIGHEST

def both_ways(value):
    return low(low_back(value))

def matmul(left, right):
    return jnp.dot(left, right, precision=highest)

def matmul_t(left, right):
    return lax.dot_general(left, right, (((1,), (1,)), ((), ())), precision=highest)

def allowed_pairs(query_pos, key_pos, length_row):

    def segment(pos):
        return jnp.where(pos < PROMPT, 0, 1 + (pos - PROMPT) // CONT).astype(jnp.int32)
    seg_query = segment(query_pos)
    seg_key = segment(key_pos)
    slot_key = ((key_pos - PROMPT) % CONT).astype(jnp.int32)
    numbers = jnp.arange(1, CONTS + 1, dtype=jnp.int32)
    key_length = lax.optimization_barrier(jnp.sum(jnp.where(seg_key[:, None] == numbers[None, :], length_row[None, :].astype(jnp.int32), 0), axis=1)).astype(jnp.int32)
    live = (seg_key == 0) | (slot_key < key_length)
    same = (seg_key[None, :] == 0) | (seg_key[None, :] == seg_query[:, None])
    return live[None, :] & same & (key_pos[None, :] <= query_pos[:, None])

def standardize(rows):
    centre = lax.optimization_barrier(jnp.mean(rows, axis=-1, keepdims=True))
    centred = rows - centre
    spread = lax.optimization_barrier(jnp.mean(centred * centred, axis=-1, keepdims=True))
    return centred * lax.rsqrt(spread + 1e-05)

def attention(queries, keys, values, allowed):
    group_len = queries.shape[0]

    def split_heads(array):
        return array.reshape(group_len, HEADS, HEAD_DIM).transpose(1, 0, 2)

    def one_head(parts):
        head_query, head_key, head_value = parts
        scores = low_back(matmul_t(head_query, head_key) * HEAD_DIM ** (-0.5))
        zeros = jnp.zeros_like(scores)
        top = lax.optimization_barrier(jnp.max(jnp.where(allowed, scores, zeros - 10000.0), axis=-1, keepdims=True))
        weights = jnp.where(allowed, jnp.exp(jnp.where(allowed, scores, zeros) - top), zeros)
        probs = weights / lax.optimization_barrier(jnp.sum(weights, axis=-1, keepdims=True))
        return matmul(low(probs), head_value)
    mixed = lax.map(jax.checkpoint(one_head), (split_heads(queries), split_heads(keys), split_heads(values)))
    return mixed.transpose(1, 0, 2).reshape(group_len, HEADS * HEAD_DIM)

def forward_group(params, hidden, allowed):
    for layer in range(LAYERS):
        w_q = params[0][layer]
        w_k = params[1][layer]
        w_v = params[2][layer]
        w_o = params[3][layer]
        w_u = params[4][layer]
        w_d = params[5][layer]
        norms = params[6][layer]
        first = low(standardize(hidden) * norms[0] + norms[1])
        queries = both_ways(matmul(first, w_q))
        keys = both_ways(matmul(first, w_k))
        values = both_ways(matmul(first, w_v))
        mixed = both_ways(attention(queries, keys, values, allowed))
        hidden = hidden + low_back(matmul_t(mixed, w_o))
        second = low(standardize(hidden) * norms[2] + norms[3])
        pre_act = low_back(matmul(second, w_u))
        active = low(jax.nn.gelu(pre_act, approximate=False))
        hidden = hidden + low_back(matmul_t(active, w_d))
    return hidden

def reference(hidden_in, cotangent, lengths, w_query, w_key, w_value, w_output, w_up, w_down, norm_params):
    params = tuple((item.astype(jnp.float32) for item in (w_query, w_key, w_value, w_output, w_up, w_down, norm_params)))
    positions = jnp.arange(GROUP, dtype=jnp.int32)

    def per_group(totals, item):
        rows, grad_rows, length_row = item
        allowed = allowed_pairs(positions, positions, length_row)
        result, pull = jax.vjp(lambda weights, inputs: forward_group(weights, inputs, allowed), params, rows)
        grad_params, grad_rows_in = pull(grad_rows)
        totals = tuple((total + grad for total, grad in zip(totals, grad_params)))
        return (totals, (result, grad_rows_in))
    zeros = tuple((jnp.zeros(item.shape, jnp.float32) for item in params))
    totals, (results, grads_in) = lax.scan(per_group, zeros, (hidden_in.astype(jnp.float32), cotangent.astype(jnp.float32), lengths.astype(jnp.int32)))
    return (results, grads_in, totals[0], totals[1], totals[2], totals[3], totals[4], totals[5], totals[6])
```

```python
import jax
import jax.numpy as jnp
from jax import lax
from jax.sharding import PartitionSpec as P

from jax.experimental import pallas as pl
from jax.experimental.pallas import tpu as pltpu

HEAD_DIM = 64
BLOCK = 128
LOG2E = 1.4426950408889634
NEG = -1e30
LAYERS = 2
PROMPT = 1024
CONTS = 8
CONT = 128


def allowed_pairs(query_pos, key_pos, length_row):

    def segment(pos):
        return jnp.where(pos < PROMPT, 0, 1 + (pos - PROMPT) // CONT)

    seg_query = segment(query_pos)
    seg_key = segment(key_pos)
    slot_key = (key_pos - PROMPT) % CONT
    numbers = jnp.arange(1, CONTS + 1, dtype=jnp.int32)
    key_length = jnp.sum(
        jnp.where(seg_key[:, None] == numbers[None, :], length_row[None, :], 0), axis=1
    )
    live = (seg_key == 0) | (slot_key < key_length)
    same = (seg_key[None, :] == 0) | (seg_key[None, :] == seg_query[:, None])
    return live[None, :] & same & (key_pos[None, :] <= query_pos[:, None])


def standardize(rows):
    centre = jnp.mean(rows, axis=-1, keepdims=True)
    centred = rows - centre
    spread = jnp.mean(centred * centred, axis=-1, keepdims=True)
    inverse = lax.rsqrt(spread + 1e-05)
    return (centred * inverse, inverse)


def smooth_act(values):
    return jax.nn.gelu(values, approximate=False)


def contract_rows(left, right):
    return lax.dot_general(
        left, right, (((0,), (0,)), ((), ())), preferred_element_type=jnp.float32
    )


def contract_cols(left, right):
    return lax.dot_general(
        left, right, (((1,), (1,)), ((), ())), preferred_element_type=jnp.float32
    )


def reduce_branch(partial_rows):
    return lax.psum_scatter(partial_rows, "tensor", scatter_dimension=1, tiled=True)


def gather_grad(rows_low):
    return lax.all_gather(rows_low, "tensor", axis=1, tiled=True)


def plain_attend(queries, keys_all, values_all, allowed, heads_here):
    tokens = queries.shape[1]
    scale = HEAD_DIM ** (-0.5)

    def one_group(parts):
        query_block, key_block, value_block, allow = parts
        head_query = query_block.reshape(tokens, heads_here, HEAD_DIM)
        head_key = key_block.reshape(key_block.shape[0], heads_here, HEAD_DIM)
        head_value = value_block.reshape(key_block.shape[0], heads_here, HEAD_DIM)
        scores = (
            jnp.einsum("qhd,khd->hqk", head_query, head_key, preferred_element_type=jnp.float32)
            * scale
        )
        zeros = jnp.zeros_like(scores)
        top = jnp.max(jnp.where(allow[None], scores, zeros - 10000.0), axis=-1, keepdims=True)
        weights = jnp.where(
            allow[None], jnp.exp(jnp.where(allow[None], scores, zeros) - top), zeros
        )
        total = jnp.sum(weights, axis=-1, keepdims=True)
        probs = (weights / total).astype(jnp.bfloat16)
        log_total = top[..., 0] + jnp.log(total[..., 0])
        mixed = jnp.einsum("hqk,khd->qhd", probs, head_value, preferred_element_type=jnp.float32)
        return (mixed.astype(jnp.bfloat16).reshape(tokens, heads_here * HEAD_DIM), log_total)

    mixed, log_total = lax.map(one_group, (queries, keys_all, values_all, allowed))
    return (mixed.reshape(-1, mixed.shape[-1]), log_total)


def plain_attend_back(queries, keys_all, values_all, grad_mixed, log_total, allowed, heads_here):
    tokens = queries.shape[1]
    scale = HEAD_DIM ** (-0.5)

    def one_group(parts):
        query_block, key_block, value_block, grad_block, log_block, allow = parts
        key_count = key_block.shape[0]
        head_query = query_block.reshape(tokens, heads_here, HEAD_DIM)
        head_key = key_block.reshape(key_count, heads_here, HEAD_DIM)
        head_value = value_block.reshape(key_count, heads_here, HEAD_DIM)
        head_grad = grad_block.reshape(tokens, heads_here, HEAD_DIM)
        scores = (
            jnp.einsum("qhd,khd->hqk", head_query, head_key, preferred_element_type=jnp.float32)
            * scale
        )
        zeros = jnp.zeros_like(scores)
        probs = jnp.where(
            allow[None],
            jnp.exp(jnp.where(allow[None], scores, zeros) - log_block[..., None]),
            zeros,
        )
        grad_probs = jnp.einsum(
            "qhd,khd->hqk", head_grad, head_value, preferred_element_type=jnp.float32
        )
        delta = jnp.sum(probs * grad_probs, axis=-1, keepdims=True)
        grad_scores = (probs * (grad_probs - delta)).astype(jnp.bfloat16)
        grad_query_rows = (
            jnp.einsum("hqk,khd->qhd", grad_scores, head_key, preferred_element_type=jnp.float32)
            * scale
        )
        key_part = (
            jnp.einsum("hqk,qhd->khd", grad_scores, head_query, preferred_element_type=jnp.float32)
            * scale
        )
        value_part = jnp.einsum(
            "hqk,qhd->khd",
            probs.astype(jnp.bfloat16),
            head_grad,
            preferred_element_type=jnp.float32,
        )
        return (
            grad_query_rows.astype(jnp.bfloat16).reshape(tokens, heads_here * HEAD_DIM),
            key_part.reshape(key_count, heads_here * HEAD_DIM),
            value_part.reshape(key_count, heads_here * HEAD_DIM),
        )

    grad_block_all = grad_mixed.reshape(queries.shape)
    grad_queries, key_part, value_part = lax.map(
        one_group, (queries, keys_all, values_all, grad_block_all, log_total, allowed)
    )
    return (grad_queries.reshape(-1, grad_queries.shape[-1]), key_part, value_part)


def norm_back(partial_rows, hat, inverse, gain, tensor_index, shard_width):
    start = tensor_index * shard_width
    whole = lax.psum(partial_rows, "tensor")
    scaled = whole * gain
    grad_full = inverse * (
        scaled
        - jnp.mean(scaled, axis=-1, keepdims=True)
        - hat * jnp.mean(scaled * hat, axis=-1, keepdims=True)
    )
    grad_cols = lax.dynamic_slice_in_dim(grad_full, start, shard_width, 1)
    whole_cols = lax.dynamic_slice_in_dim(whole, start, shard_width, 1)
    hat_cols = lax.dynamic_slice_in_dim(hat, start, shard_width, 1)
    return (grad_cols, jnp.sum(whole_cols * hat_cols, axis=0), jnp.sum(whole_cols, axis=0))


def reduce_grads(grad_q, grad_k, grad_v, grad_o, grad_u, grad_d, grad_n):
    summed = (
        lax.psum(grad_q.astype(jnp.bfloat16), ("dp", "ctx")).astype(jnp.float32),
        lax.psum(grad_k.astype(jnp.bfloat16), ("dp", "ctx")).astype(jnp.float32),
        lax.psum(grad_v.astype(jnp.bfloat16), ("dp", "ctx")).astype(jnp.float32),
        lax.psum(grad_o.astype(jnp.bfloat16), ("dp", "ctx")).astype(jnp.float32),
        lax.psum(grad_u.astype(jnp.bfloat16), ("dp", "ctx")).astype(jnp.float32),
        lax.psum(grad_d.astype(jnp.bfloat16), ("dp", "ctx")).astype(jnp.float32),
        lax.psum(grad_n.astype(jnp.bfloat16), ("dp", "ctx")).astype(jnp.float32),
    )
    n_data = lax.axis_size("dp")
    data_index = lax.axis_index("dp")
    return tuple(
        (
            lax.dynamic_slice_in_dim(
                item, data_index * (item.shape[0] // n_data), item.shape[0] // n_data, 0
            )
            for item in summed
        )
    )


def plain_body(
    hidden_in, cotangent, lengths, w_query, w_key, w_value, w_output, w_up, w_down, norm_params
):
    groups_here, tokens, shard_width = hidden_in.shape
    n_ctx = lax.axis_size("ctx")
    group_len = tokens * n_ctx
    rows_total = groups_here * tokens
    tensor_index = lax.axis_index("tensor")
    ctx_index = lax.axis_index("ctx")
    heads_here = w_query.shape[2] // HEAD_DIM
    key_pos = jnp.arange(group_len, dtype=jnp.int32)
    query_pos = ctx_index * tokens + jnp.arange(tokens, dtype=jnp.int32)
    allowed = jax.vmap(lambda length_row: allowed_pairs(query_pos, key_pos, length_row))(lengths)
    residual = hidden_in.reshape(rows_total, shard_width)
    saved = []
    for layer in range(LAYERS):
        weights = (
            lax.all_gather(w_query[layer], "dp", axis=0, tiled=True),
            lax.all_gather(w_key[layer], "dp", axis=0, tiled=True),
            lax.all_gather(w_value[layer], "dp", axis=0, tiled=True),
            lax.all_gather(w_output[layer], "dp", axis=0, tiled=True),
            lax.all_gather(w_up[layer], "dp", axis=0, tiled=True),
            lax.all_gather(w_down[layer], "dp", axis=0, tiled=True),
            lax.all_gather(norm_params[layer], "dp", axis=0, tiled=True),
        )
        residual_full, norm_full = (
            lax.all_gather(residual, "tensor", axis=1, tiled=True),
            lax.all_gather(weights[6].astype(jnp.float32), "tensor", axis=1, tiled=True),
        )
        first_hat, first_inv = standardize(residual_full)
        first_in = (first_hat * norm_full[0] + norm_full[1]).astype(jnp.bfloat16)
        queries = jnp.dot(first_in, weights[0], preferred_element_type=jnp.float32).astype(
            jnp.bfloat16
        )
        keys_local = jnp.dot(first_in, weights[1], preferred_element_type=jnp.float32).astype(
            jnp.bfloat16
        )
        values_local = jnp.dot(first_in, weights[2], preferred_element_type=jnp.float32).astype(
            jnp.bfloat16
        )
        channels = queries.shape[1]
        keys_all, values_all = (
            lax.all_gather(
                keys_local.reshape(groups_here, tokens, channels), "ctx", axis=1, tiled=True
            ),
            lax.all_gather(
                values_local.reshape(groups_here, tokens, channels), "ctx", axis=1, tiled=True
            ),
        )
        query_blocks = queries.reshape(groups_here, tokens, channels)
        mixed, log_total = plain_attend(query_blocks, keys_all, values_all, allowed, heads_here)
        middle = residual + reduce_branch(contract_cols(mixed, weights[3]))
        middle_full = lax.all_gather(middle, "tensor", axis=1, tiled=True)
        second_hat, second_inv = standardize(middle_full)
        second_in = (second_hat * norm_full[2] + norm_full[3]).astype(jnp.bfloat16)
        pre_act = jnp.dot(second_in, weights[4], preferred_element_type=jnp.float32)
        active = smooth_act(pre_act).astype(jnp.bfloat16)
        residual = middle + reduce_branch(contract_cols(active, weights[5]))
        saved.append(
            (
                weights,
                norm_full,
                first_hat,
                first_inv,
                first_in,
                query_blocks,
                keys_all,
                values_all,
                mixed,
                log_total,
                second_hat,
                second_inv,
                second_in,
                pre_act,
                active,
            )
        )
    output = residual.reshape(groups_here, tokens, shard_width)
    grad_res = cotangent.reshape(rows_total, shard_width)
    layer_grads = [None] * LAYERS
    for layer in reversed(range(LAYERS)):
        (
            weights,
            norm_full,
            first_hat,
            first_inv,
            first_in,
            query_blocks,
            keys_all,
            values_all,
            mixed,
            log_total,
            second_hat,
            second_inv,
            second_in,
            pre_act,
            active,
        ) = saved[layer]
        grad_full = gather_grad(grad_res.astype(jnp.bfloat16))
        grad_active = jnp.dot(grad_full, weights[5], preferred_element_type=jnp.float32)
        unused, pull_act = jax.vjp(smooth_act, pre_act)
        grad_pre = pull_act(grad_active)[0].astype(jnp.bfloat16)
        grad_down_w = contract_rows(grad_full, active)
        grad_up_w = contract_rows(second_in, grad_pre)
        second_part = contract_cols(grad_pre, weights[4])
        grad_mid, second_gain, second_bias = norm_back(
            second_part, second_hat, second_inv, norm_full[2], tensor_index, shard_width
        )
        grad_res = grad_res + grad_mid
        grad_full = gather_grad(grad_res.astype(jnp.bfloat16))
        grad_mixed = jnp.dot(grad_full, weights[3], preferred_element_type=jnp.float32).astype(
            jnp.bfloat16
        )
        grad_out_w = contract_rows(grad_full, mixed)
        grad_queries, key_part, value_part = plain_attend_back(
            query_blocks, keys_all, values_all, grad_mixed, log_total, allowed, heads_here
        )
        grad_keys, grad_values = (
            lax.psum_scatter(
                key_part.astype(jnp.bfloat16), "ctx", scatter_dimension=1, tiled=True
            ).astype(jnp.float32),
            lax.psum_scatter(
                value_part.astype(jnp.bfloat16), "ctx", scatter_dimension=1, tiled=True
            ).astype(jnp.float32),
        )
        grad_keys = grad_keys.reshape(rows_total, -1).astype(jnp.bfloat16)
        grad_values = grad_values.reshape(rows_total, -1).astype(jnp.bfloat16)
        grad_query_w = contract_rows(first_in, grad_queries)
        grad_key_w = contract_rows(first_in, grad_keys)
        grad_value_w = contract_rows(first_in, grad_values)
        first_part = (
            contract_cols(grad_queries, weights[0])
            + contract_cols(grad_keys, weights[1])
            + contract_cols(grad_values, weights[2])
        )
        grad_low, first_gain, first_bias = norm_back(
            first_part, first_hat, first_inv, norm_full[0], tensor_index, shard_width
        )
        grad_res = grad_res + grad_low
        grad_norm_rows = jnp.stack([first_gain, first_bias, second_gain, second_bias])
        layer_grads[layer] = reduce_grads(
            grad_query_w,
            grad_key_w,
            grad_value_w,
            grad_out_w,
            grad_up_w,
            grad_down_w,
            grad_norm_rows,
        )
    grad_input = grad_res.reshape(groups_here, tokens, shard_width)
    stacked = [
        jnp.stack([layer_grads[index][member] for index in range(LAYERS)]) for member in range(7)
    ]
    return (
        output,
        grad_input,
        stacked[0],
        stacked[1],
        stacked[2],
        stacked[3],
        stacked[4],
        stacked[5],
        stacked[6],
    )


def contract(left, right, dim_left, dim_right):
    return lax.dot_general(
        left, right, (((dim_left,), (dim_right,)), ((), ())), preferred_element_type=jnp.float32
    )


def head_stack(block):
    lanes = lax.broadcasted_iota(jnp.int32, block.shape, 1)
    zero = jnp.zeros_like(block)
    return jnp.concatenate(
        [jnp.where(lanes < HEAD_DIM, block, zero), jnp.where(lanes < HEAD_DIM, zero, block)], axis=0
    )


def head_unstack(flipped):
    picked = jnp.concatenate([flipped[:HEAD_DIM, :BLOCK], flipped[HEAD_DIM:, BLOCK:]], axis=0)
    return picked.T


def key_masks(scalars):
    slot = scalars[0]
    row = lax.broadcasted_iota(jnp.int32, (BLOCK, 2 * BLOCK), 0)
    col = lax.broadcasted_iota(jnp.int32, (BLOCK, 2 * BLOCK), 1)
    col = jnp.where(col >= BLOCK, col - BLOCK, col)
    low = []
    high = []
    for other in range(4):
        gap = BLOCK * ((slot ^ other) - slot)
        low.append(row + gap <= col)
        high.append(row - gap <= col)
    own = [(row <= col) & (row < scalars[1]), (row <= col) & (row < scalars[2])]
    return (low, high, own)


def attend_kernel(scalars, q_ref, own_ref, kv1_ref, kv2_ref, kv3_ref, out_ref, full_ref, log_ref):
    refs = (own_ref, kv1_ref, kv2_ref, kv3_ref)
    low, high, own = key_masks(scalars)
    factor = LOG2E * HEAD_DIM ** (-0.5)
    stacks = jnp.concatenate([head_stack(q_ref[i * BLOCK : (i + 1) * BLOCK]) for i in range(4)], axis=0)
    pieces = []
    wide = 2 * BLOCK
    top = [jnp.full((1, wide), NEG, jnp.float32) for _ in range(4)]
    for half in range(2):
        for other in range(4):
            keys = refs[other][half * BLOCK : (half + 1) * BLOCK, :BLOCK]
            first = half
            scores = contract(keys, stacks[first * wide :], 1, 1)
            masked = jnp.where((low, high)[half][other], scores[:, :wide], NEG)
            cols = [masked] + [scores[:, (i - first) * wide : (i - first + 1) * wide] for i in range(first + 1, 4)]
            for i in range(first, 4):
                top[i] = jnp.maximum(top[i], jnp.max(cols[i - first], axis=0, keepdims=True))
            pieces.append((refs[other], half * BLOCK, first, cols))
    for cont in range(2):
        keys = own_ref[(2 + cont) * BLOCK : (3 + cont) * BLOCK, :BLOCK]
        scores = contract(keys, stacks[(2 + cont) * wide : (3 + cont) * wide], 1, 1)
        masked = jnp.where(own[cont], scores, NEG)
        top[2 + cont] = jnp.maximum(top[2 + cont], jnp.max(masked, axis=0, keepdims=True))
        pieces.append((own_ref, (2 + cont) * BLOCK, 2 + cont, [masked]))
    top = [item * factor for item in top]
    total = [jnp.zeros((1, wide), jnp.float32) for _ in range(4)]
    mixed = [jnp.zeros((BLOCK, wide), jnp.float32) for _ in range(4)]
    for ref, start, first, cols in pieces:
        weights = []
        for i, item in enumerate(cols):
            weight = jnp.exp2(item * factor - top[first + i])
            total[first + i] = total[first + i] + jnp.sum(weight, axis=0, keepdims=True)
            weights.append(weight.astype(jnp.bfloat16))
        joined = weights[0] if len(weights) == 1 else jnp.concatenate(weights, axis=1)
        values = ref[start : start + BLOCK, BLOCK:]
        part = contract(values, joined, 0, 0)
        for i in range(len(cols)):
            mixed[first + i] = mixed[first + i] + part[:, i * wide : (i + 1) * wide]
    for i in range(4):
        done = mixed[i] * (1.0 / total[i])
        done = head_unstack(done)
        full_ref[i * BLOCK : (i + 1) * BLOCK, :] = done
        out_ref[i * BLOCK : (i + 1) * BLOCK, :] = done.astype(jnp.bfloat16)
        log_ref[0, i : i + 1, :] = top[i] + jnp.log2(total[i])


def kv_specs(pairs):
    half = pairs // 2
    same = lambda h, s: (0, h)
    swapped = lambda h, s: (0, (h + half) % pairs)
    return [
        pl.BlockSpec((4 * BLOCK, 2 * BLOCK), same),
        pl.BlockSpec((2 * BLOCK, 2 * BLOCK), same),
        pl.BlockSpec((2 * BLOCK, 2 * BLOCK), swapped),
        pl.BlockSpec((2 * BLOCK, 2 * BLOCK), swapped),
    ]


def attend(scalars, queries, own, kv1, kv2, kv3):
    tokens, channels = queries.shape
    pairs = channels // BLOCK
    row = pl.BlockSpec((tokens, BLOCK), lambda h, s: (0, h))
    return pl.pallas_call(
        attend_kernel,
        grid_spec=pltpu.PrefetchScalarGridSpec(
            num_scalar_prefetch=1,
            grid=(pairs,),
            in_specs=[row] + kv_specs(pairs),
            out_specs=[row, row, pl.BlockSpec((1, 8, 2 * BLOCK), lambda h, s: (h, 0, 0))],
        ),
        out_shape=[
            jax.ShapeDtypeStruct((tokens, channels), jnp.bfloat16),
            jax.ShapeDtypeStruct((tokens, channels), jnp.float32),
            jax.ShapeDtypeStruct((pairs, 8, 2 * BLOCK), jnp.float32),
        ],
        compiler_params=pltpu.CompilerParams(vmem_limit_bytes=48 * 2**20),
        name="attend",
    )(scalars, queries, own, kv1, kv2, kv3)


def attend_back_kernel(
    scalars, q_ref, g_ref, o_ref, log_ref, own_ref, kv1_ref, kv2_ref, kv3_ref,
    dq_ref, d0_ref, d1_ref, d2_ref, d3_ref,
):
    refs = (own_ref, kv1_ref, kv2_ref, kv3_ref)
    outs = (d0_ref, d1_ref, d2_ref, d3_ref)
    low, high, own = key_masks(scalars)
    scale = HEAD_DIM ** (-0.5)
    factor = LOG2E * scale
    wide = 2 * BLOCK
    blocks = [slice(i * BLOCK, (i + 1) * BLOCK) for i in range(4)]
    stacks = jnp.concatenate([head_stack(q_ref[b]) for b in blocks], axis=0)
    grads = jnp.concatenate([head_stack(g_ref[b]) for b in blocks], axis=0)
    deltas = []
    logs = []
    for i, b in enumerate(blocks):
        flipped = (g_ref[b].astype(jnp.float32) * o_ref[b]).T
        deltas.append(
            jnp.concatenate(
                [
                    jnp.sum(flipped[:HEAD_DIM], axis=0, keepdims=True),
                    jnp.sum(flipped[HEAD_DIM:], axis=0, keepdims=True),
                ],
                axis=1,
            )
        )
        logs.append(log_ref[0, i : i + 1, :])
    dq = [jnp.zeros((BLOCK, wide), jnp.float32) for _ in range(4)]

    def part(ref, out, start, first, last, mask):
        keys = ref[start : start + BLOCK, :BLOCK]
        values = ref[start : start + BLOCK, BLOCK:]
        scores = contract(keys, stacks[first * wide : last * wide], 1, 1)
        grad_probs = contract(values, grads[first * wide : last * wide], 1, 1)
        probs = []
        grad_scores = []
        for i in range(first, last):
            at = slice((i - first) * wide, (i - first + 1) * wide)
            prob = jnp.exp2(scores[:, at] * factor - logs[i])
            if i == first:
                prob = jnp.where(mask, prob, 0.0)
            probs.append(prob.astype(jnp.bfloat16))
            grad_scores.append((prob * (grad_probs[:, at] - deltas[i])).astype(jnp.bfloat16))
        prob = probs[0] if len(probs) == 1 else jnp.concatenate(probs, axis=1)
        grad_score = grad_scores[0] if len(probs) == 1 else jnp.concatenate(grad_scores, axis=1)
        out[start : start + BLOCK, BLOCK:] = contract(prob, grads[first * wide : last * wide], 1, 0).astype(jnp.bfloat16)
        out[start : start + BLOCK, :BLOCK] = (
            contract(grad_score, stacks[first * wide : last * wide], 1, 0) * scale
        ).astype(jnp.bfloat16)
        back = contract(keys, grad_score, 0, 0)
        for i in range(first, last):
            dq[i] = dq[i] + back[:, (i - first) * wide : (i - first + 1) * wide]

    for half in range(2):
        for other in range(4):
            part(refs[other], outs[other], half * BLOCK, half, 4, (low, high)[half][other])
    for cont in range(2):
        part(own_ref, d0_ref, (2 + cont) * BLOCK, 2 + cont, 3 + cont, own[cont])
    for i, b in enumerate(blocks):
        dq_ref[b, :] = (head_unstack(dq[i]) * scale).astype(jnp.bfloat16)


def attend_back(scalars, queries, grad_mixed, mixed, logs, own, kv1, kv2, kv3):
    tokens, channels = queries.shape
    pairs = channels // BLOCK
    row = pl.BlockSpec((tokens, BLOCK), lambda h, s: (0, h))
    log = pl.BlockSpec((1, 8, 2 * BLOCK), lambda h, s: (h, 0, 0))
    low = jnp.bfloat16
    return pl.pallas_call(
        attend_back_kernel,
        grid_spec=pltpu.PrefetchScalarGridSpec(
            num_scalar_prefetch=1,
            grid=(pairs,),
            in_specs=[row, row, row, log] + kv_specs(pairs),
            out_specs=[row] + kv_specs(pairs),
        ),
        out_shape=[
            jax.ShapeDtypeStruct((tokens, channels), low),
            jax.ShapeDtypeStruct(own.shape, low),
            jax.ShapeDtypeStruct(kv1.shape, low),
            jax.ShapeDtypeStruct(kv2.shape, low),
            jax.ShapeDtypeStruct(kv3.shape, low),
        ],
        compiler_params=pltpu.CompilerParams(vmem_limit_bytes=48 * 2**20),
        name="attend_back",
    )(scalars, queries, grad_mixed, mixed, logs, own, kv1, kv2, kv3)


def gelu_pair(value):
    half = 0.5 + 0.5 * lax.erf(value * (2.0 ** -0.5))
    density = jnp.exp2(value * value * (-0.5 * LOG2E)) * 0.3989422804014327
    return (value * half, half + value * density)


def up_kernel(x_ref, w1_ref, w2_ref, *rest):
    act_ref, slope_ref = rest[-2:]
    depth = w1_ref.shape[0]
    x = x_ref[...]
    step = 256
    for at in range(0, w1_ref.shape[1], step):
        pre = jnp.dot(x[:, :depth], w1_ref[:, at : at + step], preferred_element_type=jnp.float32)
        pre = pre + jnp.dot(x[:, depth:], w2_ref[:, at : at + step], preferred_element_type=jnp.float32)
        act, slope = gelu_pair(pre)
        act_ref[:, at : at + step] = act.astype(jnp.bfloat16)
        slope_ref[:, at : at + step] = slope.astype(jnp.bfloat16)


def up_half(x, w1, w2, half, held=None, tile=1024):
    tokens, width = x.shape
    hidden = w1.shape[1]
    wide = pl.BlockSpec((w1.shape[0], tile), lambda j: (0, j))
    out = pl.BlockSpec((tokens, tile), lambda j: (half, j))
    shape = jax.ShapeDtypeStruct((2 * tokens, hidden), jnp.bfloat16)
    extra = () if held is None else tuple(held)
    return pl.pallas_call(
        up_kernel,
        grid=(hidden // tile,),
        in_specs=[pl.BlockSpec((tokens, width), lambda j: (0, 0)), wide, wide] + [pl.BlockSpec(memory_space=pl.ANY)] * len(extra),
        out_specs=[out, out],
        out_shape=[shape, shape],
        input_output_aliases={3: 0, 4: 1} if extra else {},
        compiler_params=pltpu.CompilerParams(vmem_limit_bytes=48 * 2**20),
        name="up_gelu",
    )(x, w1, w2, *extra)


def pre_kernel(x_ref, w1_ref, w2_ref, slope_ref, *rest):
    out_ref = rest[-1]
    depth = w1_ref.shape[0]
    x = x_ref[...]
    step = 256
    for at in range(0, w1_ref.shape[1], step):
        grad = jnp.dot(x[:, :depth], w1_ref[:, at : at + step], preferred_element_type=jnp.float32)
        grad = grad + jnp.dot(x[:, depth:], w2_ref[:, at : at + step], preferred_element_type=jnp.float32)
        out_ref[:, at : at + step] = (grad * slope_ref[:, at : at + step].astype(jnp.float32)).astype(jnp.bfloat16)


def pre_half(x, w1, w2, slope, half, held=None, tile=1024):
    tokens, width = x.shape
    hidden = w1.shape[1]
    wide = pl.BlockSpec((w1.shape[0], tile), lambda j: (0, j))
    out = pl.BlockSpec((tokens, tile), lambda j: (half, j))
    shape = jax.ShapeDtypeStruct((2 * tokens, hidden), jnp.bfloat16)
    extra = () if held is None else (held,)
    return pl.pallas_call(
        pre_kernel,
        grid=(hidden // tile,),
        in_specs=[pl.BlockSpec((tokens, width), lambda j: (0, 0)), wide, wide, out] + [pl.BlockSpec(memory_space=pl.ANY)] * len(extra),
        out_specs=out,
        out_shape=shape,
        input_output_aliases={4: 0} if extra else {},
        compiler_params=pltpu.CompilerParams(vmem_limit_bytes=48 * 2**20),
        name="grad_pre",
    )(x, w1, w2, slope, *extra)


SWAP_CORE = [(0, 1), (1, 0), (2, 3), (3, 2)]
SWAP_X = [(0, 2), (2, 0), (1, 3), (3, 1)]
SWAP_Y = [(0, 1), (1, 0)]
SWAP_Z = [(0, 1), (1, 0), (2, 3), (3, 2)]
SWAP_FAR = [(0, 2), (2, 0), (1, 3), (3, 1)]
ALL_AXES = ("dp", "ctx", "tensor")


def core_swap(item):
    return lax.ppermute(item, "dp", SWAP_CORE)


def x_swap(item):
    return lax.ppermute(item, "dp", SWAP_X)


def y_swap(item):
    return lax.ppermute(item, "tensor", SWAP_Y)


def z_swap(item):
    return lax.ppermute(item, "ctx", SWAP_Z)


FLIPS = (0, 2, 1, 3)


def take_blocks(rows, order):
    width = rows.shape[-1] // 4
    return jnp.concatenate(
        [lax.dynamic_slice_in_dim(rows, at * width, width, rows.ndim - 1) for at in order], axis=-1
    )


def to_own_order(rows, data_index):
    return take_blocks(rows, [data_index ^ flip for flip in FLIPS])


def from_own_order(rows, data_index):
    turned = 2 * (data_index % 2) + data_index // 2
    return take_blocks(rows, [turned ^ flip for flip in FLIPS])


def exchange_pairs(there, bits):
    flip_i, flip_core, flip_y = bits
    pairs = []
    for x in range(2):
        for core in range(2):
            for z in range(4):
                for y in range(2):
                    source = ((2 * x + core) * 4 + z) * 2 + y
                    core_to = (z // 2) ^ flip_core
                    z_to = 2 * core + ((z % 2) ^ flip_i)
                    y_to = y ^ flip_y
                    target = ((2 * x + core_to) * 4 + z_to) * 2 + y_to
                    pairs.append((source, target) if there else (target, source))
    return pairs


ALL_BITS = [(a, e, b) for b in range(2) for a in range(2) for e in range(2)]


def to_slots(shard, place):
    _, core, z, y = place
    block = CONT
    half = shard.shape[2]
    low = shard.astype(jnp.bfloat16)
    rows = jnp.zeros((4 * block, 2 * half), jnp.bfloat16)
    for bits in ALL_BITS:
        flip_i, flip_core, flip_y = bits
        slot = 2 * (y ^ flip_y) + ((z // 2) ^ flip_core)
        at = jnp.where(z == 1, 3 - slot, slot)
        piece = lax.dynamic_slice(low, ((z % 2) ^ flip_i, at * block, 0), (1, block, half))[0]
        got = lax.ppermute(piece, ALL_AXES, exchange_pairs(True, bits))
        z_from = 2 * (core ^ flip_core) + ((z % 2) ^ flip_i)
        rows = lax.dynamic_update_slice(rows, got, (z_from * block, (y ^ flip_y) * half))
    return rows


def from_slots(rows, place):
    _, core, z, y = place
    block = CONT
    half = rows.shape[1] // 2
    low = rows.astype(jnp.bfloat16)
    shard = jnp.zeros((2, 4 * block, half), jnp.bfloat16)
    for bits in ALL_BITS:
        flip_i, flip_core, flip_y = bits
        z_from = 2 * (core ^ flip_core) + ((z % 2) ^ flip_i)
        piece = lax.dynamic_slice(low, (z_from * block, (y ^ flip_y) * half), (block, half))
        got = lax.ppermute(piece, ALL_AXES, exchange_pairs(False, bits))
        slot = 2 * (y ^ flip_y) + ((z // 2) ^ flip_core)
        at = jnp.where(z == 1, 3 - slot, slot)
        shard = lax.dynamic_update_slice(shard, got[None], ((z % 2) ^ flip_i, at * block, 0))
    return shard.astype(jnp.float32)


def pick(bit, if_zero, if_one):
    return jnp.where(bit == 0, if_zero, if_one)


def join_kv(key_part, value_part):
    rows, channels = key_part.shape
    both = jnp.stack(
        [
            key_part.reshape(rows, channels // BLOCK, BLOCK),
            value_part.reshape(rows, channels // BLOCK, BLOCK),
        ],
        axis=2,
    )
    return both.reshape(rows, 2 * channels)


def part_kv(both):
    rows, wide = both.shape
    split = both.reshape(rows, wide // (2 * BLOCK), 2, BLOCK)
    return split[:, :, 0].reshape(rows, wide // 2), split[:, :, 1].reshape(rows, wide // 2)


def gather_attn(w_query, w_key, w_value, w_output, z_bit):
    own = jnp.concatenate([w_query, join_kv(w_key, w_value), w_output], axis=1)
    across = x_swap(own)
    sent = y_swap(pick(z_bit, own, across))
    swapped = z_swap(sent)
    other_own = pick(z_bit, sent, swapped)
    other_across = pick(z_bit, swapped, sent)
    sib_own, sib_across = core_swap(own), core_swap(across)
    sib_sent, sib_swapped = core_swap(sent), core_swap(swapped)
    sib_other_own = pick(z_bit, sib_sent, sib_swapped)
    sib_other_across = pick(z_bit, sib_swapped, sib_sent)
    left = (own, across, sib_own, sib_across)
    right = (other_own, other_across, sib_other_own, sib_other_across)
    width = w_query.shape[1]

    def whole(start, stop):
        return jnp.concatenate(
            [
                jnp.concatenate([a[:, start:stop], b[:, start:stop]], axis=1)
                for a, b in zip(left, right)
            ],
            axis=0,
        )

    return whole(0, width), whole(width, 3 * width), whole(3 * width, 4 * width)


def gather_wide(w_up, w_down, z_bit):
    sent = x_swap(pick(z_bit, w_up, w_down))
    swapped = z_swap(sent)
    up = jnp.concatenate([w_up, pick(z_bit, sent, swapped)], axis=0)
    down = jnp.concatenate([w_down, pick(z_bit, swapped, sent)], axis=0)
    return up, core_swap(up), down, core_swap(down)


def sum_over_z(part, z):
    inward = lax.ppermute(part, "ctx", [(0, 1), (3, 2)])
    pair = (part.astype(jnp.float32) + inward.astype(jnp.float32)).astype(jnp.bfloat16)
    other = lax.ppermute(pair, "ctx", [(1, 2), (2, 1)])
    total = (pair.astype(jnp.float32) + other.astype(jnp.float32)).astype(jnp.bfloat16)
    outward = lax.ppermute(total, "ctx", [(1, 0), (2, 3)])
    return jnp.where((z == 1) | (z == 2), total, outward)


def add_low(left, right):
    return (left.astype(jnp.float32) + right.astype(jnp.float32)).astype(jnp.bfloat16)


def reduce_wide(left, right, z):
    width = left.shape[1] // 4
    cols = [left[:, r * width : (r + 1) * width] for r in range(4)]
    part = [contract_rows(item, right) for item in (cols[3], cols[1], cols[2], cols[0])]
    sent_across = core_swap(part[0].astype(jnp.bfloat16))
    across = add_low(part[1], sent_across)
    got = x_swap(across)
    sent_own = core_swap(part[2].astype(jnp.bfloat16))
    own = (part[3] + sent_own.astype(jnp.float32) + got.astype(jnp.float32)).astype(jnp.bfloat16)
    return sum_over_z(own, z)


def reduce_attn(left, right, half, z):
    rows = left.shape[1]
    core_part = contract_rows(left[:, rows // 2 :], right).astype(jnp.bfloat16)
    got = core_swap(core_part)
    mine = add_low(contract_rows(left[:, : rows // 2], right), got)
    mine = add_low(mine[:, :half], y_swap(mine[:, half:]))
    mine = add_low(mine[: rows // 4], x_swap(mine[rows // 4 :]))
    return sum_over_z(mine, z)


def norm_back_rows(grad, hat, inverse, gain):
    scaled = grad * gain
    back = inverse * (
        scaled
        - jnp.mean(scaled, axis=-1, keepdims=True)
        - hat * jnp.mean(scaled * hat, axis=-1, keepdims=True)
    )
    return back, jnp.sum(grad * hat, axis=0), jnp.sum(grad, axis=0)


def sum_everywhere(item):
    item = item + core_swap(item)
    item = item + y_swap(item)
    item = item + x_swap(item)
    item = item + z_swap(item)
    return item + lax.ppermute(item, "ctx", SWAP_FAR)


def fast_body(
    hidden_in, cotangent, lengths, w_query, w_key, w_value, w_output, w_up, w_down, norm_params
):
    data_index = lax.axis_index("dp")
    z = lax.axis_index("ctx")
    y = lax.axis_index("tensor")
    core = data_index % 2
    place = (data_index // 2, core, z, y)
    z_bit = z % 2
    slot = 2 * y + core
    bf16 = jnp.bfloat16
    half = w_query.shape[2]
    tokens = 4 * CONT
    prompt_here = 2 * CONT

    both_lengths = lengths.astype(jnp.float32)
    own_lengths = jnp.where(z // 2 == core, both_lengths, core_swap(both_lengths))
    row_lengths = lax.dynamic_slice_in_dim(own_lengths, z % 2, 1, 0)[0]
    scalars = jnp.stack(
        [
            slot,
            lax.dynamic_slice_in_dim(row_lengths, slot, 1, 0)[0].astype(jnp.int32),
            lax.dynamic_slice_in_dim(row_lengths, slot + 4, 1, 0)[0].astype(jnp.int32),
        ]
    ).astype(jnp.int32)

    hidden = to_own_order(to_slots(hidden_in, place), data_index).astype(jnp.float32)
    norms = lax.all_gather(norm_params, "dp", axis=1, tiled=True)
    norms = lax.all_gather(norms.astype(jnp.float32), "tensor", axis=2, tiled=True)
    norms = to_own_order(norms, data_index)
    attn = [
        gather_attn(w_query[i], w_key[i], w_value[i], w_output[i], z_bit) for i in range(LAYERS)
    ]
    wide = [gather_wide(w_up[i], w_down[i], z_bit) for i in range(LAYERS)]
    saved = []
    for layer in range(LAYERS):
        wq, wkv, wo = attn[layer]
        up1, up2, down1, down2 = wide[layer]
        gains = norms[layer]
        first_hat, first_inv = standardize(hidden)
        first = (first_hat * gains[0] + gains[1]).astype(bf16)
        kv = jnp.dot(first, wkv, preferred_element_type=jnp.float32).astype(bf16)
        kv_prompt = kv[:prompt_here]
        kv2 = y_swap(kv_prompt)
        kv1 = core_swap(kv_prompt)
        kv3 = core_swap(kv2)
        queries = jnp.dot(first, wq, preferred_element_type=jnp.float32).astype(bf16)
        mixed, mixed_full, logs = attend(scalars, queries, kv, kv1, kv2, kv3)
        middle = hidden + contract_cols(mixed, wo)
        second_hat, second_inv = standardize(middle)
        second = (second_hat * gains[2] + gains[3]).astype(bf16)
        second_other = y_swap(second)
        held = up_half(second, up1, up2, 0)
        act, slope = up_half(second_other, up1, up2, 1, held)
        other = jnp.concatenate(
            [contract_cols(act[tokens:], down1), contract_cols(act[tokens:], down2)], axis=1
        ).astype(bf16)
        back = y_swap(other)
        mine = jnp.concatenate(
            [contract_cols(act[:tokens], down1), contract_cols(act[:tokens], down2)], axis=1
        )
        saved.append(
            (first_hat, first_inv, first, queries, kv, kv1, kv2, kv3, mixed, mixed_full, logs,
             second_hat, second_inv, second, second_other, act, slope)
        )
        hidden = middle + mine + back.astype(jnp.float32)
    output = from_slots(from_own_order(hidden.astype(bf16), data_index), place)

    grad = to_own_order(to_slots(cotangent, place), data_index).astype(jnp.float32)
    results = [None] * LAYERS
    for layer in reversed(range(LAYERS)):
        (first_hat, first_inv, first, queries, kv, kv1, kv2, kv3, mixed, mixed_full, logs,
         second_hat, second_inv, second, second_other, act, slope) = saved[layer]
        wq, wkv, wo = attn[layer]
        up1, up2, down1, down2 = wide[layer]
        gains = norms[layer]
        low = grad.astype(bf16)
        low_other = y_swap(low)
        held = pre_half(low, down1, down2, slope, 0)
        grad_pre = pre_half(low_other, down1, down2, slope, 1, held)
        other = jnp.concatenate(
            [contract_cols(grad_pre[tokens:], up1), contract_cols(grad_pre[tokens:], up2)], axis=1
        ).astype(bf16)
        back = y_swap(other)
        mine = jnp.concatenate(
            [contract_cols(grad_pre[:tokens], up1), contract_cols(grad_pre[:tokens], up2)], axis=1
        )
        grad_down_w = reduce_wide(jnp.concatenate([low, low_other], axis=0), act, z)
        grad_up_w = reduce_wide(jnp.concatenate([second, second_other], axis=0), grad_pre, z)
        grad_second = mine + back.astype(jnp.float32)
        grad_mid, second_gain, second_bias = norm_back_rows(
            grad_second, second_hat, second_inv, gains[2]
        )
        grad = grad + grad_mid
        low = grad.astype(bf16)
        grad_mixed = jnp.dot(low, wo, preferred_element_type=jnp.float32).astype(bf16)
        grad_out_w = reduce_attn(low, mixed, half, z)
        dq, d0, d1, d2, d3 = attend_back(
            scalars, queries, grad_mixed, mixed_full, logs, kv, kv1, kv2, kv3
        )
        d2 = add_low(d2, core_swap(d3))
        from_core = core_swap(d1)
        from_y = y_swap(d2)
        prompt_part = (
            d0[:prompt_here].astype(jnp.float32)
            + from_core.astype(jnp.float32)
            + from_y.astype(jnp.float32)
        ).astype(bf16)
        dkv = jnp.concatenate([prompt_part, d0[prompt_here:]], axis=0)
        grad_query_w = reduce_attn(first, dq, half, z)
        grad_kv_w = reduce_attn(first, dkv, 2 * half, z)
        grad_first = contract_cols(dq, wq) + contract_cols(dkv, wkv)
        grad_low, first_gain, first_bias = norm_back_rows(
            grad_first, first_hat, first_inv, gains[0]
        )
        grad = grad + grad_low
        grad_norm = from_own_order(
            jnp.stack([first_gain, first_bias, second_gain, second_bias]), data_index
        )
        grad_norm = sum_everywhere(grad_norm)
        grad_norm = lax.dynamic_slice(grad_norm, (data_index, y * half), (1, half))
        grad_key_w, grad_value_w = part_kv(grad_kv_w)
        results[layer] = (
            grad_query_w, grad_key_w, grad_value_w, grad_out_w, grad_up_w, grad_down_w, grad_norm
        )
    grad_input = from_slots(from_own_order(grad.astype(bf16), data_index), place)
    stacked = [
        jnp.stack([results[i][member].astype(jnp.float32) for i in range(LAYERS)])
        for member in range(7)
    ]
    return (output, grad_input, *stacked)


def solution(mesh):
    sizes = dict(mesh.shape)
    fits = (sizes["dp"], sizes["ctx"], sizes["tensor"]) == (4, 4, 2)
    body = fast_body if fits else plain_body
    in_specs = (
        P("dp", "ctx", "tensor"),
        P("dp", "ctx", "tensor"),
        P("dp", None),
        P(None, "dp", "tensor"),
        P(None, "dp", "tensor"),
        P(None, "dp", "tensor"),
        P(None, "dp", "tensor"),
        P(None, "dp", "tensor"),
        P(None, "dp", "tensor"),
        P(None, "dp", "tensor"),
    )
    out_specs = (
        P("dp", "ctx", "tensor"),
        P("dp", "ctx", "tensor"),
        P(None, "dp", "tensor"),
        P(None, "dp", "tensor"),
        P(None, "dp", "tensor"),
        P(None, "dp", "tensor"),
        P(None, "dp", "tensor"),
        P(None, "dp", "tensor"),
        P(None, "dp", "tensor"),
    )
    return jax.shard_map(body, mesh=mesh, in_specs=in_specs, out_specs=out_specs, check_vma=False)
```
